32 devices in a mesh: gx: 4 (over z), gy: 8 (over y, x, core).
Axes of the slice: x: 2, y: 2, z: 4, core: 2. Of those that a mesh axis runs over, the one named last changes fastest.
Arguments:
- pixel_adjoint: float32 [4, 32, 4096], P(None, None, ('gx', 'gy')), may hold values from -6 to 6
- pixel_owner: int32 [4, 4096, 1], P(None, ('gx', 'gy')), may hold values from 0 to 31; in each aligned block of 128 rows (0 to 127, 128 to 255, ..., all dimensions but the last counted through in order) at most 8 rows name the same one
- pixel_column: int32 [4, 4096], P(None, ('gx', 'gy')), may hold values from 0 to 1023
- pixel_level: int32 [4, 4096], P(None, ('gx', 'gy')), may hold values from 0 to 24
- wind_x: float32 [4, 32, 1024], P(None, 'gx', 'gy'), may hold values from -0.45 to 0.45
- wind_y: float32 [4, 32, 1024], P(None, 'gx', 'gy'), may hold values from -0.45 to 0.45
- diffusivity: float32 [39, 32, 1024], P(None, 'gx', 'gy'), may hold values from 0.1 to 10
- prior_emission: float32 [2, 32, 1024], P(None, 'gx', 'gy'), may hold values from 0.01 to 0.1
- region_map: int32 [32, 1024], P('gx', 'gy'), may hold values from 0 to 255, as said below
Outputs:
- adjoint_out: float32 [2, 40, 32, 1024], P(None, None, 'gx', 'gy')
- emission_gradient: float32 [2, 256], P(None, ('gx', 'gy'))
The draws below stay inside these ranges and needn't reach their ends.
Inputs may be any that keep to these rules, and one draw needn't show every extreme that they name: `pixel_owner`: within the 128 entries of one device in one step no owner is named more than 8 times, a bound that some block reaches. `region_map`: constant on aligned blocks of 2 rows by 4 columns; every region covers exactly 16 such blocks.
All inputs are finite; a program needn't handle non-finite values.
Results may differ from the reference program's by a relative error of at most 0.00014.
Values sent between devices are 32-bit elements; how exact they have to be, the bound alone decides.
A program may use at most 64 MiB of HBM per device.

```python
import math
import jax
import jax.numpy as jnp
import numpy as np
from jax import lax

CX = 8
CY = 128
LEV = 40
S = 2
AKL = 16
STEPS = 4
PIX = 128
NX = 32
NY = 1024
NPIX = 4096
CAP = 8
NREG = 256
N_GY = 8
DEVICES = 32


def draw_region_map(key, part):
    rows_blk = NX // 2
    cols_blk = NY // 4
    order = jax.random.permutation(key, rows_blk * cols_blk) % NREG
    blocks = order.reshape(rows_blk, cols_blk).astype(jnp.int32)
    return jnp.repeat(jnp.repeat(blocks, 2, axis=0), 4, axis=1)


def plant(values, key, smallest, top_value):
    longest = values.shape.index(max(values.shape))
    spots = []
    for shift in (0, 1):
        where = [jax.random.randint(jax.random.fold_in(key, axis), (), 0, length) for axis, length in enumerate(values.shape)]
        where[longest] = (where[longest] + shift) % values.shape[longest]
        spots.append(tuple(where))
    return values.at[spots[0]].set(smallest).at[spots[1]].set(top_value)


def steps_of(rng, extent, split, low, largest):
    level, own = 1.0, jax.random.fold_in(rng, 6)
    for position, blocks in split:
        draws = jnp.exp(jax.random.uniform(jax.random.fold_in(own, position), (blocks,), jnp.float32, low / len(split), largest / len(split)))
        level = level * jnp.repeat(draws, extent[position] // blocks).reshape([-1 if axis == position else 1 for axis in range(len(extent))])
    return level


def shared_out(stream_key, own, number, rows, count, top, most, skew):
    order = jax.random.permutation(stream_key, count)
    packed, usual = portions_of(count, rows * top, most, skew, True), portions_of(count, rows * top, most, skew, False)
    places = jnp.arange(count)

    def named(lengths, rotation):
        used = int((lengths > 0).sum())
        fixed = max(1, used // 4)
        passed = fixed + (places - fixed + rotation * (used - fixed)) % max(1, count - fixed)
        return jnp.zeros((count,), jnp.int32).at[order[jnp.where(places < fixed, places, passed)]].set(jnp.asarray(lengths, jnp.int32))

    lengths = jnp.where(number % 4 == 0, named(packed, number // 4), named(usual, number - number // 4 - 1))
    mixed = jax.random.permutation(jax.random.fold_in(own, 3), count)
    giver, receiver = mixed[0:count // 2 * 2:2], mixed[1:count // 2 * 2:2]
    room = jnp.minimum(lengths[giver] - 1, most - lengths[receiver]) // 2
    room = jnp.where((giver == order[0]) | (receiver == order[0]) | (lengths[receiver] == 0), 0, jnp.maximum(room, 0))
    passed = jax.random.randint(jax.random.fold_in(own, 4), (count // 2,), 0, 1 << 20) % (room + 1)
    lengths = lengths.at[giver].add(-passed).at[receiver].add(passed)
    items = jnp.searchsorted(jnp.cumsum(lengths), jnp.arange(rows * top), side="right").astype(jnp.int32)
    grid = items.reshape(top, rows).T
    grid = grid[jax.random.permutation(jax.random.fold_in(own, 1), rows)]
    rotation = jax.random.randint(jax.random.fold_in(own, 2), (rows, 1), 0, top)
    return jnp.take_along_axis(grid, (jnp.arange(top)[None, :] + rotation) % top, axis=1)


def portions_of(amount, total, reach, skew, full):
    weights = [(1 << 20) // math.isqrt(rank ** skew) + 1 for rank in range(1, amount + 1)]
    largest = reach if full else min(reach, max(-(-total // amount), total * weights[0] // sum(weights)))
    least = 1 if total - largest >= amount - 1 else 0
    given, surplus = [largest] + [least] * (amount - 1), total - largest - least * (amount - 1)
    while surplus > 0:
        candidates = [i for i in range(1, amount) if given[i] < largest] or [i for i in range(1, amount) if given[i] < reach]
        whole, remaining = sum([weights[i] for i in candidates]), surplus
        for i in candidates:
            more = min(reach - given[i], max(1, remaining * weights[i] // whole), surplus)
            given[i] = given[i] + more
            surplus = surplus - more
    return np.array(given)


def gaussian(stream_key, shape, deviation, bound, split=(), held_as=jnp.bfloat16):
    entries = deviation * jax.random.normal(stream_key, shape, jnp.float32)
    if split:
        entries = entries * steps_of(stream_key, shape, split, -0.22, 0.18)
    return jnp.clip(entries, -bound, bound).astype(held_as)


def setup_inputs(seed: int = 0) -> dict:
    keys = jax.random.split(jax.random.key(seed), 10)
    pixel_adjoint = gaussian(keys[0], (STEPS, S * AKL, NPIX), 1.0, 6.0, ((2, 32),), jnp.float32)
    pixel_owner_keys = jax.random.split(jax.random.fold_in(keys[1], 1), STEPS * NPIX // PIX)
    pixel_owner_turns = jax.random.permutation(jax.random.fold_in(keys[1], 3), STEPS * NPIX // PIX)
    pixel_owner = jax.vmap(lambda own, number: shared_out(jax.random.fold_in(keys[1], 2), own, number, PIX, DEVICES, 1, CAP, 2))(pixel_owner_keys, pixel_owner_turns).reshape((STEPS, NPIX, 1))
    pixel_column = plant(jax.random.randint(keys[2], (STEPS, NPIX), 0, CX * CY), jax.random.fold_in(keys[2], 1), 0, (CX * CY) - 1).astype(jnp.int32)
    pixel_level = plant(jax.random.randint(keys[3], (STEPS, NPIX), 0, LEV - AKL + 1), jax.random.fold_in(keys[3], 1), 0, LEV - AKL).astype(jnp.int32)
    wind_x = jnp.clip(jax.random.uniform(keys[4], (STEPS, NX, NY), jnp.float32, -0.45, 0.45) * steps_of(keys[4], (STEPS, NX, NY), ((1, 4), (2, 8)), -0.4, 0.0), -0.45, 0.45)
    wind_y = jnp.clip(jax.random.uniform(keys[5], (STEPS, NX, NY), jnp.float32, -0.45, 0.45) * steps_of(keys[5], (STEPS, NX, NY), ((1, 4), (2, 8)), -0.4, 0.0), -0.45, 0.45)
    diffusivity = jnp.clip(jnp.exp(math.log(10.0) - 4.6051702 * jax.random.uniform(keys[6], (LEV - 1, NX, NY), jnp.float32) ** steps_of(keys[6], (LEV - 1, NX, NY), ((1, 4), (2, 8)), -0.2, 0.2)), 0.1, 10.0)
    prior_emission = jnp.clip(jnp.exp(math.log(0.1) - 2.3025851 * jax.random.uniform(keys[7], (S, NX, NY), jnp.float32) ** steps_of(keys[7], (S, NX, NY), ((1, 4), (2, 8)), -0.2, 0.2)), 0.01, 0.1)
    region_map = draw_region_map(jax.random.fold_in(keys[9], 71), 0)
    return {"pixel_adjoint": pixel_adjoint, "pixel_owner": pixel_owner, "pixel_column": pixel_column, "pixel_level": pixel_level, "wind_x": wind_x, "wind_y": wind_y, "diffusivity": diffusivity, "prior_emission": prior_emission, "region_map": region_map}


def spread(payload, column, start, species, levels, kernel, cells):
    offset = jnp.arange(levels, dtype=jnp.int32)[:, None] - start[None, :]
    inside = (offset >= 0) & (offset < kernel)
    kernel_row = jnp.clip(offset, 0, kernel - 1)
    values = payload.reshape(species, kernel, -1)
    picked = jnp.take_along_axis(values, jnp.broadcast_to(kernel_row[None], (species, levels, kernel_row.shape[1])), axis=1)
    profile = jnp.where(inside[None], picked, 0.0)
    forcing = jnp.zeros((species * levels, cells), jnp.float32)
    return forcing.at[:, column].add(profile.reshape(species * levels, -1))


def transpose_advect(padded, wind_pad):
    eastward = jnp.maximum(wind_pad[0], 0.0)
    westward = jnp.maximum(-wind_pad[0], 0.0)
    northward = jnp.maximum(wind_pad[1], 0.0)
    southward = jnp.maximum(-wind_pad[1], 0.0)
    remain = 1.0 - (eastward + westward + northward + southward)[1:-1, 1:-1]
    moved = padded[:, :, 1:-1, 1:-1] * remain
    moved = moved + (eastward * padded)[:, :, 2:, 1:-1] + (westward * padded)[:, :, :-2, 1:-1]
    moved = moved + (northward * padded)[:, :, 1:-1, 2:] + (southward * padded)[:, :, 1:-1, :-2]
    return moved


def factor(diffusivity):
    edge = jnp.zeros_like(diffusivity[:1])
    below = jnp.concatenate([edge, diffusivity], axis=0)
    above = jnp.concatenate([diffusivity, edge], axis=0)

    def sweep(carried, inputs):
        below_row, above_row = inputs
        inverse_row = 1.0 / (1.0 + below_row + above_row + below_row * carried)
        ratio_row = -above_row * inverse_row
        return ratio_row, (ratio_row, inverse_row)

    end_state, (ratios, inverses) = lax.scan(sweep, jnp.zeros_like(edge[0]), (below, above))
    return below, ratios, inverses


def solve(rhs, below, ratios, inverses):
    stacked = jnp.moveaxis(rhs, 1, 0)

    def forward(carried, inputs):
        rhs_row, below_row, inverse_row = inputs
        reduced = (rhs_row + below_row * carried) * inverse_row
        return reduced, reduced

    end_state, reduced_all = lax.scan(forward, jnp.zeros_like(stacked[0]), (stacked, below, inverses))

    def backward(carried, inputs):
        reduced_row, ratio_row = inputs
        result = reduced_row - ratio_row * carried
        return result, result

    top_state, solved = lax.scan(backward, jnp.zeros_like(stacked[0]), (reduced_all, ratios), reverse=True)
    return jnp.moveaxis(solved, 0, 1)


def reference(pixel_adjoint, pixel_owner, pixel_column, pixel_level, wind_x, wind_y, diffusivity, prior_emission, region_map):
    cells = NX * NY
    below, ratios, inverses = factor(diffusivity)
    winds = jnp.pad(jnp.stack([wind_x, wind_y]), ((0, 0), (0, 0), (1, 1), (1, 1)))
    adjoint = jnp.zeros((S, LEV, NX, NY), jnp.float32)
    surface_sum = jnp.zeros((S, NX, NY), jnp.float32)
    for moment in reversed(range(STEPS)):
        owners = pixel_owner[moment, :, 0]
        column = pixel_column[moment]
        grid_row = (owners // N_GY) * CX + column // CY
        grid_col = (owners % N_GY) * CY + column % CY
        flat = (grid_row * NY + grid_col).astype(jnp.int32)
        forcing = spread(pixel_adjoint[moment], flat, pixel_level[moment], S, LEV, AKL, cells).reshape(S, LEV, NX, NY)
        forced = adjoint + forcing
        padded = jnp.pad(forced, ((0, 0), (0, 0), (1, 1), (1, 1)))
        moved = transpose_advect(padded, winds[:, moment])
        adjoint = solve(moved, below, ratios, inverses)
        surface_sum = surface_sum + prior_emission * adjoint[:, 0]
    gradient = jax.ops.segment_sum(surface_sum.reshape(S, -1).T, region_map.reshape(-1), num_segments=NREG).T
    return (adjoint, gradient)
```

```python
import functools

import jax
import jax.numpy as jnp
from jax import lax
from jax.experimental import pallas as pl
from jax.experimental.pallas import tpu as pltpu
from jax.sharding import PartitionSpec as P

REG_DEV = 8
MESH = pl.DeviceIdType.MESH
F32 = jnp.float32
BF16 = jnp.bfloat16


def halves(value):
    high = value.astype(BF16)
    low = (value - high.astype(F32)).astype(BF16)
    return high, low


def dot_nt(a, b):
    return lax.dot_general(a, b, (((1,), (1,)), ((), ())), preferred_element_type=F32)


def kernel(
    dims,
    adj_ref,
    owner_ref,
    column_ref,
    level_ref,
    wx_ref,
    wy_ref,
    diff_ref,
    prior_ref,
    region_ref,
    state,
    grad_ref,
    table,
    send,
    recv,
    inv_ref,
    coup_ref,
    ratio_ref,
    forcing,
    forced,
    moved,
    row_out,
    row_in,
    col_out,
    col_in,
    surf,
    gsend,
    grecv,
    pix_send,
    pix_recv,
    halo_send,
    halo_recv,
    g_send,
    g_recv,
):
    nx, ny, species, levels, akl, steps, rows, cols, pixels, slots = dims
    n = nx * ny
    planes = species * levels
    gx, gy = lax.axis_index("gx"), lax.axis_index("gy")
    me = gx * ny + gy

    def partner(i):
        other = lax.rem(me + i, n)
        return other, (lax.div(other, ny), lax.rem(other, ny))

    row_in[...] = jnp.zeros(row_in.shape, F32)
    col_in[...] = jnp.zeros(col_in.shape, F32)
    barrier = pltpu.get_barrier_semaphore()

    def greet(i, carry):
        other, place = partner(i)
        pl.semaphore_signal(barrier, inc=1, device_id=place, device_id_type=MESH)
        return carry

    lax.fori_loop(1, n, greet, 0)

    def pack(k):
        table[...] = jnp.zeros((128, pixels), F32)
        for s in range(species):
            table[s * levels : s * levels + akl, :] = adj_ref[k, s * akl : (s + 1) * akl, :]
        table[planes : planes + 1, :] = column_ref[k : k + 1, :].astype(F32)
        table[planes + 1 : planes + 2, :] = level_ref[k : k + 1, :].astype(F32)
        owner = owner_ref[k : k + 1, :].astype(F32)
        along = jnp.broadcast_to(owner, (pixels, pixels))
        down = along.T
        first = lax.broadcasted_iota(jnp.int32, (pixels, pixels), 0)
        second = lax.broadcasted_iota(jnp.int32, (pixels, pixels), 1)
        earlier = jnp.where((along == down) & (first < second), 1.0, 0.0)
        slot = jnp.sum(earlier, axis=0, keepdims=True)
        position = (owner * slots + slot).astype(jnp.int32)
        place = lax.broadcasted_iota(jnp.int32, (n * slots, pixels), 0)
        hits = jnp.where(place == position, 1.0, 0.0).astype(BF16)
        high, low = halves(table[...])
        send[k] = dot_nt(hits, high) + dot_nt(hits, low)

    def pixel_copy(k, i):
        other, place = partner(i)
        return pltpu.make_async_remote_copy(
            src_ref=send.at[k, pl.ds(pl.multiple_of(other * slots, slots), slots)],
            dst_ref=recv.at[k, pl.ds(pl.multiple_of(me * slots, slots), slots)],
            send_sem=pix_send.at[k],
            recv_sem=pix_recv.at[k],
            device_id=place,
            device_id_type=MESH,
        )

    def pixel_all(k):
        _, place = partner(1)
        part = pl.ds(0, (n - 1) * slots)
        return pltpu.make_async_remote_copy(
            src_ref=send.at[k, part],
            dst_ref=recv.at[k, part],
            send_sem=pix_send.at[k],
            recv_sem=pix_recv.at[k],
            device_id=place,
            device_id_type=MESH,
        )

    def send_pixels(k):
        def go(i, carry):
            pixel_copy(k, i).start()
            return carry

        lax.fori_loop(1, n, go, 0)
        mine = pl.ds(pl.multiple_of(me * slots, slots), slots)
        recv[k, mine, :] = send[k, mine, :]

    pack(steps - 1)
    pl.semaphore_wait(barrier, n - 1)
    send_pixels(steps - 1)
    for k in reversed(range(steps - 1)):
        pack(k)
        send_pixels(k)

    ratio = jnp.zeros((rows, cols), F32)
    for level in range(levels):
        below = diff_ref[level - 1] if level else jnp.zeros((rows, cols), F32)
        above = diff_ref[level] if level < levels - 1 else jnp.zeros((rows, cols), F32)
        inverse = 1.0 / (1.0 + below + above + below * ratio)
        ratio = -above * inverse
        here = slice(level * rows, (level + 1) * rows)
        inv_ref[here, :] = inverse
        coup_ref[here, :] = below * inverse
        ratio_ref[here, :] = ratio
    surf[...] = jnp.zeros(surf.shape, F32)
    state[...] = jnp.zeros(state.shape, F32)

    lane = lax.broadcasted_iota(jnp.int32, (rows, cols), 1)
    sub = lax.broadcasted_iota(jnp.int32, (rows, cols), 0)

    def spread(k):
        pixel_all(k).wait_recv()
        total = [None] * rows
        chunk = min(256, n * slots)
        for first in range(0, n * slots, chunk):
            got = recv[k, first : first + chunk, :]
            spot = lax.broadcasted_iota(jnp.int32, got.shape, 1)
            column = jnp.broadcast_to(got[:, planes : planes + 1], got.shape).astype(jnp.int32)
            level = jnp.broadcast_to(got[:, planes + 1 : planes + 2], got.shape).astype(jnp.int32)
            profile = jnp.where(spot < planes, got, 0.0)
            bit = 1
            while bit <= levels - akl:
                profile = jnp.where((level & bit) != 0, pltpu.roll(profile, bit, 1), profile)
                bit *= 2
            high, low = halves(profile.T[:planes])
            both = jnp.concatenate([high, low], axis=0)
            for x in range(0, rows, 2):
                hits = jnp.concatenate(
                    [
                        jnp.where(column == spot + (x + d) * cols, 1.0, 0.0).astype(BF16)
                        for d in range(2)
                    ],
                    axis=1,
                )
                out = jnp.dot(both, hits, preferred_element_type=F32)
                out = out[:planes] + out[planes:]
                for d in range(2):
                    piece = out[:, d * cols : (d + 1) * cols]
                    total[x + d] = piece if total[x + d] is None else total[x + d] + piece
        for x in range(rows):
            forcing[pl.ds(x, planes, stride=rows), :] = total[x]

    has = (gx < nx - 1, gx > 0, gy < ny - 1, gy > 0)
    comes = (gx > 0, gx < nx - 1, gy > 0, gy < ny - 1)
    goes = (
        (jnp.minimum(gx + 1, nx - 1), gy),
        (jnp.maximum(gx - 1, 0), gy),
        (gx, jnp.minimum(gy + 1, ny - 1)),
        (gx, jnp.maximum(gy - 1, 0)),
    )

    def halo(k, side):
        source, target = (row_out, row_in) if side < 2 else (col_out, col_in)
        return pltpu.make_async_remote_copy(
            src_ref=source.at[k, side % 2],
            dst_ref=target.at[k, side % 2],
            send_sem=halo_send.at[k, side],
            recv_sem=halo_recv.at[k, side],
            device_id=goes[side],
            device_id_type=MESH,
        )

    spread(steps - 1)

    def step(turn, carry):
        k = steps - 1 - turn
        wx, wy = wx_ref[k], wy_ref[k]
        ahead_x, back_x = jnp.maximum(-wx, 0.0), jnp.maximum(wx, 0.0)
        ahead_y, back_y = jnp.maximum(-wy, 0.0), jnp.maximum(wy, 0.0)
        forced[...] = state[...] + forcing[...]
        row_out[k, 0] = forced[pl.ds(rows - 1, planes, stride=rows), :] * ahead_x[rows - 1 : rows]
        row_out[k, 1] = forced[pl.ds(0, planes, stride=rows), :] * back_x[0:1]
        for side in (0, 1):
            pl.when(has[side])(lambda side=side: halo(k, side).start())
        up = jnp.zeros((rows, cols), F32)
        down = jnp.zeros((rows, cols), F32)
        for j in range(planes):
            cell = forced[j * rows : (j + 1) * rows, :]
            up = jnp.where(lane == j, pltpu.roll(ahead_y * cell, (j + 1) % cols, 1), up)
            down = jnp.where(lane == j, pltpu.roll(back_y * cell, j, 1) if j else back_y * cell, down)
        col_out[k, 0] = up
        col_out[k, 1] = down
        for side in (2, 3):
            pl.when(has[side])(lambda side=side: halo(k, side).start())
        remain = 1.0 - (ahead_x + back_x + ahead_y + back_y)
        ahead_x_in = jnp.where(sub > 0, pltpu.roll(ahead_x, 1, 0), 0.0)
        back_x_in = jnp.where(sub < rows - 1, pltpu.roll(back_x, rows - 1, 0), 0.0)
        ahead_y_in = jnp.where(lane > 0, pltpu.roll(ahead_y, 1, 1), 0.0)
        back_y_in = jnp.where(lane < cols - 1, pltpu.roll(back_y, cols - 1, 1), 0.0)
        for j in range(planes):
            cell = forced[j * rows : (j + 1) * rows, :]
            moved[j * rows : (j + 1) * rows, :] = (
                cell * remain
                + ahead_x_in * pltpu.roll(cell, 1, 0)
                + back_x_in * pltpu.roll(cell, rows - 1, 0)
                + ahead_y_in * pltpu.roll(cell, 1, 1)
                + back_y_in * pltpu.roll(cell, cols - 1, 1)
            )

        @pl.when(k > 0)
        def _():
            spread(jnp.maximum(k - 1, 0))

        for side in range(4):
            pl.when(comes[side])(lambda side=side: halo(k, side).wait_recv())
        moved[pl.ds(0, planes, stride=rows), :] += row_in[k, 0]
        moved[pl.ds(rows - 1, planes, stride=rows), :] += row_in[k, 1]
        up = col_in[k, 0]
        down = col_in[k, 1]
        for s in range(species):
            value = jnp.zeros((rows, cols), F32)
            for level in range(levels):
                j = s * levels + level
                here = slice(j * rows, (j + 1) * rows)
                flat = slice(level * rows, (level + 1) * rows)
                edge = jnp.where(lane == 0, pltpu.roll(up, (cols - j) % cols, 1) if j else up, 0.0)
                edge = jnp.where(lane == cols - 1, pltpu.roll(down, cols - 1 - j, 1), edge)
                value = (moved[here, :] + edge) * inv_ref[flat, :] + coup_ref[flat, :] * value
                moved[here, :] = value
            value = jnp.zeros((rows, cols), F32)
            for level in reversed(range(levels)):
                j = s * levels + level
                here = slice(j * rows, (j + 1) * rows)
                flat = slice(level * rows, (level + 1) * rows)
                value = moved[here, :] - ratio_ref[flat, :] * value
                state[here, :] = value
            surf[s] += prior_ref[s] * value
        return carry

    lax.fori_loop(0, steps, step, 0)

    region = region_ref[...]
    hits, parts = [], []
    sums = [surf[s] + pltpu.roll(surf[s], rows - 1, 0) for s in range(species)]
    for x in range(0, rows, 2):
        reg = region[x : x + 1]
        owner = lax.broadcasted_iota(jnp.int32, (n, cols), 0)
        hits.append(jnp.where(owner == lax.shift_right_logical(reg, 3), 1.0, 0.0).astype(BF16))
        place = lax.broadcasted_iota(jnp.int32, (REG_DEV, cols), 0)
        same = place == (reg & (REG_DEV - 1))
        blocks = [jnp.where(same, sums[s][x : x + 1], 0.0) for s in range(species)]
        blocks.append(jnp.zeros((128 - species * REG_DEV, cols), F32))
        parts.append(jnp.concatenate(blocks, axis=0))
    hits = jnp.concatenate(hits, axis=1)
    high, low = halves(jnp.concatenate(parts, axis=1))
    gsend[...] = (dot_nt(hits, high) + dot_nt(hits, low)).reshape(n, 1, 128)

    def grad_copy(i):
        other, place = partner(i)
        return pltpu.make_async_remote_copy(
            src_ref=gsend.at[other],
            dst_ref=grecv.at[me],
            send_sem=g_send,
            recv_sem=g_recv,
            device_id=place,
            device_id_type=MESH,
        )

    def go(i, carry):
        grad_copy(i).start()
        return carry

    lax.fori_loop(1, n, go, 0)
    grecv[me] = gsend[me]
    for k in range(steps):
        pixel_all(k).wait_send()
        for side in range(4):
            pl.when(has[side])(lambda side=side, k=k: halo(k, side).wait_send())
    _, place = partner(1)
    everything = pltpu.make_async_remote_copy(
        src_ref=gsend.at[pl.ds(0, n - 1)],
        dst_ref=grecv.at[pl.ds(0, n - 1)],
        send_sem=g_send,
        recv_sem=g_recv,
        device_id=place,
        device_id_type=MESH,
    )
    everything.wait_send()
    everything.wait_recv()
    total = jnp.sum(grecv[...], axis=0)
    for s in range(species):
        grad_ref[s : s + 1, :] = total[:, s * REG_DEV : (s + 1) * REG_DEV]


def local(nx, ny, *args):
    adj, owner, column, level, wx, wy, diff, prior, region = args
    steps, rows, cols = wx.shape
    levels, species = diff.shape[0] + 1, prior.shape[0]
    pixels, akl = adj.shape[2], adj.shape[1] // species
    n = nx * ny
    slots = -(-(2 * pixels // n) // 8) * 8
    planes = species * levels
    dims = (nx, ny, species, levels, akl, steps, rows, cols, pixels, slots)
    vmem = pl.BlockSpec(memory_space=pltpu.VMEM)
    tile = (planes * rows, cols)
    state, grad = pl.pallas_call(
        functools.partial(kernel, dims),
        out_shape=(
            jax.ShapeDtypeStruct(tile, F32),
            jax.ShapeDtypeStruct((species, REG_DEV), F32),
        ),
        in_specs=[vmem] * 9,
        out_specs=(vmem, vmem),
        scratch_shapes=[
            pltpu.VMEM((128, pixels), F32),
            pltpu.VMEM((steps, n * slots, 128), F32),
            pltpu.VMEM((steps, n * slots, 128), F32),
            pltpu.VMEM((levels * rows, cols), F32),
            pltpu.VMEM((levels * rows, cols), F32),
            pltpu.VMEM((levels * rows, cols), F32),
            pltpu.VMEM(tile, F32),
            pltpu.VMEM(tile, F32),
            pltpu.VMEM(tile, F32),
            pltpu.VMEM((steps, 2, planes, cols), F32),
            pltpu.VMEM((steps, 2, planes, cols), F32),
            pltpu.VMEM((steps, 2, rows, cols), F32),
            pltpu.VMEM((steps, 2, rows, cols), F32),
            pltpu.VMEM((species, rows, cols), F32),
            pltpu.VMEM((n, 1, 128), F32),
            pltpu.VMEM((n, 1, 128), F32),
            pltpu.SemaphoreType.DMA((steps,)),
            pltpu.SemaphoreType.DMA((steps,)),
            pltpu.SemaphoreType.DMA((steps, 4)),
            pltpu.SemaphoreType.DMA((steps, 4)),
            pltpu.SemaphoreType.DMA,
            pltpu.SemaphoreType.DMA,
        ],
        compiler_params=pltpu.CompilerParams(
            collective_id=0, has_side_effects=True, vmem_limit_bytes=40 * 1024 * 1024
        ),
    )(adj, owner.reshape(steps, pixels), column, level, wx, wy, diff, prior, region)
    return state.reshape(species, levels, rows, cols), grad


def solution(mesh):
    in_specs = (
        P(None, None, ("gx", "gy")),
        P(None, ("gx", "gy"), None),
        P(None, ("gx", "gy")),
        P(None, ("gx", "gy")),
        P(None, "gx", "gy"),
        P(None, "gx", "gy"),
        P(None, "gx", "gy"),
        P(None, "gx", "gy"),
        P("gx", "gy"),
    )
    out_specs = (P(None, None, "gx", "gy"), P(None, ("gx", "gy")))
    body = functools.partial(local, mesh.shape["gx"], mesh.shape["gy"])
    return jax.shard_map(body, mesh=mesh, in_specs=in_specs, out_specs=out_specs, check_vma=False)
```

```python
import functools

import jax
import jax.numpy as jnp
from jax import lax
from jax.experimental import pallas as pl
from jax.experimental.pallas import tpu as pltpu
from jax.sharding import PartitionSpec as P

REG_DEV = 8
MESH = pl.DeviceIdType.MESH
F32 = jnp.float32
BF16 = jnp.bfloat16


def halves(value):
    high = value.astype(BF16)
    low = (value - high.astype(F32)).astype(BF16)
    return high, low


def dot_nt(a, b):
    return lax.dot_general(a, b, (((1,), (1,)), ((), ())), preferred_element_type=F32)


def kernel(
    dims,
    *refs,
):
    sources, refs = refs[:9], refs[9:]
    state, grad_ref = refs[:2]
    inside, refs = refs[2:11], refs[11:]
    adj_ref, owner_ref, column_ref, level_ref, wx_ref, wy_ref, diff_ref, prior_ref, region_ref = inside
    moves = list(zip(sources, inside))
    (
    table,
    send,
    recv,
    inv_ref,
    coup_ref,
    ratio_ref,
    forcing,
    forced,
    moved,
    row_out,
    row_in,
    col_out,
    col_in,
    surf,
    gsend,
    grecv,
    pix_send,
    pix_recv,
    halo_send,
    halo_recv,
    g_send,
    g_recv,
    in_sem,
    ) = refs
    nx, ny, species, levels, akl, steps, rows, cols, pixels, slots = dims
    n = nx * ny
    planes = species * levels
    width = species * akl + 8
    gx, gy = lax.axis_index("gx"), lax.axis_index("gy")
    me = gx * ny + gy

    def partner(dx, dy):
        px, py = gx + dx, gy + dy
        px = jnp.where(px >= nx, px - nx, px)
        py = jnp.where(py >= ny, py - ny, py)
        return px * ny + py, (px, py)

    turns = [(dx, dy) for dx in range(nx) for dy in range(ny)][1:]

    row_in[...] = jnp.zeros(row_in.shape, F32)
    col_in[...] = jnp.zeros(col_in.shape, F32)
    loads = [pltpu.make_async_copy(a, b, in_sem.at[i]) for i, (a, b) in enumerate(moves)]
    for load in loads:
        load.start()
    table[...] = jnp.zeros(table.shape, F32)
    barrier = pltpu.get_barrier_semaphore()

    for turn in turns:
        pl.semaphore_signal(barrier, inc=1, device_id=partner(*turn)[1], device_id_type=MESH)

    for i in range(4):
        loads[i].wait()

    def hits_of(k):
        owner = owner_ref[k : k + 1, :].astype(F32)
        along = jnp.broadcast_to(owner, (pixels, pixels))
        down = along.T
        first = lax.broadcasted_iota(jnp.int32, (pixels, pixels), 0)
        second = lax.broadcasted_iota(jnp.int32, (pixels, pixels), 1)
        earlier = jnp.where((along == down) & (first < second), 1.0, 0.0)
        slot = jnp.sum(earlier, axis=0, keepdims=True)
        position = (owner * slots + slot).astype(jnp.int32)
        place = lax.broadcasted_iota(jnp.int32, (n * slots, pixels), 0)
        return jnp.where(place == position, 1.0, 0.0).astype(BF16)

    def pack(t, group):
        for i, k in enumerate(group):
            at = width * i
            table[t, at : at + species * akl, i * pixels : (i + 1) * pixels] = adj_ref[k]
            at = at + species * akl
            codes = jnp.concatenate([column_ref[k : k + 1, :], level_ref[k : k + 1, :]], axis=0)
            table[t, at : at + 2, i * pixels : (i + 1) * pixels] = codes.astype(F32)
        hits = jnp.concatenate([hits_of(k) for k in group], axis=1)
        high, low = halves(table[t, :, : len(group) * pixels])
        send[t] = dot_nt(hits, high) + dot_nt(hits, low)

    def pixel_copy(t, turn):
        other, place = partner(*turn)
        return pltpu.make_async_remote_copy(
            src_ref=send.at[t, pl.ds(pl.multiple_of(other * slots, slots), slots)],
            dst_ref=recv.at[t, pl.ds(pl.multiple_of(me * slots, slots), slots)],
            send_sem=pix_send.at[t],
            recv_sem=pix_recv.at[t],
            device_id=place,
            device_id_type=MESH,
        )

    def pixel_all(t):
        part = pl.ds(0, (n - 1) * slots)
        return pltpu.make_async_remote_copy(
            src_ref=send.at[t, part],
            dst_ref=recv.at[t, part],
            send_sem=pix_send.at[t],
            recv_sem=pix_recv.at[t],
            device_id=partner(*turns[0])[1],
            device_id_type=MESH,
        )

    def send_pixels(t):
        for turn in turns:
            pixel_copy(t, turn).start()
        mine = pl.ds(pl.multiple_of(me * slots, slots), slots)
        recv[t, mine, :] = send[t, mine, :]

    pack(0, (steps - 1,))
    pl.semaphore_wait(barrier, n - 1)
    send_pixels(0)
    pack(1, tuple(range(steps - 1)))
    send_pixels(1)
    for load in loads[4:]:
        load.wait()

    ratio = jnp.zeros((rows, cols), F32)
    for level in range(levels):
        below = diff_ref[level - 1] if level else jnp.zeros((rows, cols), F32)
        above = diff_ref[level] if level < levels - 1 else jnp.zeros((rows, cols), F32)
        inverse = 1.0 / (1.0 + below + above + below * ratio)
        ratio = -above * inverse
        here = slice(level * rows, (level + 1) * rows)
        inv_ref[here, :] = inverse
        coup_ref[here, :] = below * inverse
        ratio_ref[here, :] = ratio
    surf[...] = jnp.zeros(surf.shape, F32)
    state[...] = jnp.zeros(state.shape, F32)

    lane = lax.broadcasted_iota(jnp.int32, (rows, cols), 1)
    sub = lax.broadcasted_iota(jnp.int32, (rows, cols), 0)

    def spread(t, k):
        if t == 0:
            pixel_all(0).wait_recv()
        total = [None] * rows
        chunk = min(256, n * slots)
        for first in range(0, n * slots, chunk):
            got = recv[t, first : first + chunk, :]
            if t:
                got = pltpu.roll(got, lax.rem(128 - width * k, 128), 1)
            spot = lax.broadcasted_iota(jnp.int32, got.shape, 1)
            column = jnp.broadcast_to(got[:, width - 8 : width - 7], got.shape).astype(jnp.int32)
            level = jnp.broadcast_to(got[:, width - 7 : width - 6], got.shape).astype(jnp.int32)
            profile = jnp.where(spot < akl, got, 0.0)
            for s in range(1, species):
                place = s * levels
                there = (spot >= place) & (spot < place + akl)
                profile = jnp.where(there, pltpu.roll(got, place - s * akl, 1), profile)
            bit = 1
            while bit <= levels - akl:
                profile = jnp.where((level & bit) != 0, pltpu.roll(profile, bit, 1), profile)
                bit *= 2
            high, low = halves(profile.T[:planes])
            both = jnp.concatenate([high, low], axis=0)
            for x in range(0, rows, 2):
                hits = jnp.concatenate(
                    [
                        jnp.where(column == spot + (x + d) * cols, 1.0, 0.0).astype(BF16)
                        for d in range(2)
                    ],
                    axis=1,
                )
                out = jnp.dot(both, hits, preferred_element_type=F32)
                out = out[:planes] + out[planes:]
                for d in range(2):
                    piece = out[:, d * cols : (d + 1) * cols]
                    total[x + d] = piece if total[x + d] is None else total[x + d] + piece
        for x in range(rows):
            forcing[pl.ds(x, planes, stride=rows), :] = total[x]

    has = (gx < nx - 1, gx > 0, gy < ny - 1, gy > 0)
    comes = (gx > 0, gx < nx - 1, gy > 0, gy < ny - 1)
    goes = (
        (jnp.minimum(gx + 1, nx - 1), gy),
        (jnp.maximum(gx - 1, 0), gy),
        (gx, jnp.minimum(gy + 1, ny - 1)),
        (gx, jnp.maximum(gy - 1, 0)),
    )

    def halo(k, side):
        source, target = (row_out, row_in) if side < 2 else (col_out, col_in)
        return pltpu.make_async_remote_copy(
            src_ref=source.at[k, side % 2],
            dst_ref=target.at[k, side % 2],
            send_sem=halo_send.at[k, side],
            recv_sem=halo_recv.at[k, side],
            device_id=goes[side],
            device_id_type=MESH,
        )

    spread(0, 0)

    def step(turn, carry):
        k = steps - 1 - turn
        wx, wy = wx_ref[k], wy_ref[k]
        ahead_x, back_x = jnp.maximum(-wx, 0.0), jnp.maximum(wx, 0.0)
        ahead_y, back_y = jnp.maximum(-wy, 0.0), jnp.maximum(wy, 0.0)
        forced[...] = state[...] + forcing[...]
        row_out[k, 0] = forced[pl.ds(rows - 1, planes, stride=rows), :] * ahead_x[rows - 1 : rows]
        row_out[k, 1] = forced[pl.ds(0, planes, stride=rows), :] * back_x[0:1]
        for side in (0, 1):
            pl.when(has[side])(lambda side=side: halo(k, side).start())
        up = jnp.zeros((rows, cols), F32)
        down = jnp.zeros((rows, cols), F32)
        for j in range(planes):
            cell = forced[j * rows : (j + 1) * rows, :]
            up = jnp.where(lane == j, pltpu.roll(ahead_y * cell, (j + 1) % cols, 1), up)
            down = jnp.where(lane == j, pltpu.roll(back_y * cell, j, 1) if j else back_y * cell, down)
        col_out[k, 0] = up
        col_out[k, 1] = down
        for side in (2, 3):
            pl.when(has[side])(lambda side=side: halo(k, side).start())
        remain = 1.0 - (ahead_x + back_x + ahead_y + back_y)
        ahead_x_in = jnp.where(sub > 0, pltpu.roll(ahead_x, 1, 0), 0.0)
        back_x_in = jnp.where(sub < rows - 1, pltpu.roll(back_x, rows - 1, 0), 0.0)
        ahead_y_in = jnp.where(lane > 0, pltpu.roll(ahead_y, 1, 1), 0.0)
        back_y_in = jnp.where(lane < cols - 1, pltpu.roll(back_y, cols - 1, 1), 0.0)
        for j in range(planes):
            cell = forced[j * rows : (j + 1) * rows, :]
            moved[j * rows : (j + 1) * rows, :] = (
                cell * remain
                + ahead_x_in * pltpu.roll(cell, 1, 0)
                + back_x_in * pltpu.roll(cell, rows - 1, 0)
                + ahead_y_in * pltpu.roll(cell, 1, 1)
                + back_y_in * pltpu.roll(cell, cols - 1, 1)
            )

        @pl.when(k > 0)
        def _():
            pl.when(k == steps - 1)(lambda: pixel_all(1).wait_recv())
            spread(1, jnp.maximum(k - 1, 0))

        for side in range(4):
            pl.when(comes[side])(lambda side=side: halo(k, side).wait_recv())
        moved[pl.ds(0, planes, stride=rows), :] += row_in[k, 0]
        moved[pl.ds(rows - 1, planes, stride=rows), :] += row_in[k, 1]
        up = col_in[k, 0]
        down = col_in[k, 1]
        for s in range(species):
            value = jnp.zeros((rows, cols), F32)
            for level in range(levels):
                j = s * levels + level
                here = slice(j * rows, (j + 1) * rows)
                flat = slice(level * rows, (level + 1) * rows)
                edge = jnp.where(lane == 0, pltpu.roll(up, (cols - j) % cols, 1) if j else up, 0.0)
                edge = jnp.where(lane == cols - 1, pltpu.roll(down, cols - 1 - j, 1), edge)
                value = (moved[here, :] + edge) * inv_ref[flat, :] + coup_ref[flat, :] * value
                moved[here, :] = value
            value = jnp.zeros((rows, cols), F32)
            for level in reversed(range(levels)):
                j = s * levels + level
                here = slice(j * rows, (j + 1) * rows)
                flat = slice(level * rows, (level + 1) * rows)
                value = moved[here, :] - ratio_ref[flat, :] * value
                state[here, :] = value
            surf[s] += prior_ref[s] * value
        return carry

    lax.fori_loop(0, steps, step, 0)

    region = region_ref[...]
    hits, parts = [], []
    sums = [surf[s] + pltpu.roll(surf[s], rows - 1, 0) for s in range(species)]
    for x in range(0, rows, 2):
        reg = region[x : x + 1]
        owner = lax.broadcasted_iota(jnp.int32, (n, cols), 0)
        hits.append(jnp.where(owner == lax.shift_right_logical(reg, 3), 1.0, 0.0).astype(BF16))
        place = lax.broadcasted_iota(jnp.int32, (REG_DEV, cols), 0)
        same = place == (reg & (REG_DEV - 1))
        blocks = [jnp.where(same, sums[s][x : x + 1], 0.0) for s in range(species)]
        blocks.append(jnp.zeros((128 - species * REG_DEV, cols), F32))
        parts.append(jnp.concatenate(blocks, axis=0))
    hits = jnp.concatenate(hits, axis=1)
    high, low = halves(jnp.concatenate(parts, axis=1))
    gsend[...] = (dot_nt(hits, high) + dot_nt(hits, low)).reshape(n, 1, 128)

    for turn in turns:
        other, place = partner(*turn)
        pltpu.make_async_remote_copy(
            src_ref=gsend.at[other],
            dst_ref=grecv.at[me],
            send_sem=g_send,
            recv_sem=g_recv,
            device_id=place,
            device_id_type=MESH,
        ).start()
    grecv[me] = gsend[me]
    for t in range(2):
        pixel_all(t).wait_send()
    for k in range(steps):
        for side in range(4):
            pl.when(has[side])(lambda side=side, k=k: halo(k, side).wait_send())
    everything = pltpu.make_async_remote_copy(
        src_ref=gsend.at[pl.ds(0, n - 1)],
        dst_ref=grecv.at[pl.ds(0, n - 1)],
        send_sem=g_send,
        recv_sem=g_recv,
        device_id=partner(*turns[0])[1],
        device_id_type=MESH,
    )
    everything.wait_send()
    everything.wait_recv()
    total = jnp.sum(grecv[...], axis=0)
    for s in range(species):
        grad_ref[s : s + 1, :] = total[:, s * REG_DEV : (s + 1) * REG_DEV]


def local(nx, ny, *args):
    adj, owner, column, level, wx, wy, diff, prior, region = args
    steps, rows, cols = wx.shape
    levels, species = diff.shape[0] + 1, prior.shape[0]
    pixels, akl = adj.shape[2], adj.shape[1] // species
    n = nx * ny
    slots = -(-(2 * pixels // n) // 8) * 8
    planes = species * levels
    dims = (nx, ny, species, levels, akl, steps, rows, cols, pixels, slots)
    vmem = pl.BlockSpec(memory_space=pltpu.VMEM)
    tile = (planes * rows, cols)
    operands = (adj, owner.reshape(steps, pixels), column, level, wx, wy, diff, prior, region)
    state, grad = pl.pallas_call(
        functools.partial(kernel, dims),
        out_shape=(
            jax.ShapeDtypeStruct(tile, F32),
            jax.ShapeDtypeStruct((species, REG_DEV), F32),
        ),
        in_specs=[pl.BlockSpec(memory_space=pltpu.HBM)] * 9,
        out_specs=(vmem, vmem),
        scratch_shapes=[
            *[pltpu.VMEM(a.shape, a.dtype) for a in operands],
            pltpu.VMEM((2, 128, (steps - 1) * pixels), F32),
            pltpu.VMEM((2, n * slots, 128), F32),
            pltpu.VMEM((2, n * slots, 128), F32),
            pltpu.VMEM((levels * rows, cols), F32),
            pltpu.VMEM((levels * rows, cols), F32),
            pltpu.VMEM((levels * rows, cols), F32),
            pltpu.VMEM(tile, F32),
            pltpu.VMEM(tile, F32),
            pltpu.VMEM(tile, F32),
            pltpu.VMEM((steps, 2, planes, cols), F32),
            pltpu.VMEM((steps, 2, planes, cols), F32),
            pltpu.VMEM((steps, 2, rows, cols), F32),
            pltpu.VMEM((steps, 2, rows, cols), F32),
            pltpu.VMEM((species, rows, cols), F32),
            pltpu.VMEM((n, 1, 128), F32),
            pltpu.VMEM((n, 1, 128), F32),
            pltpu.SemaphoreType.DMA((2,)),
            pltpu.SemaphoreType.DMA((2,)),
            pltpu.SemaphoreType.DMA((steps, 4)),
            pltpu.SemaphoreType.DMA((steps, 4)),
            pltpu.SemaphoreType.DMA,
            pltpu.SemaphoreType.DMA,
            pltpu.SemaphoreType.DMA((9,)),
        ],
        compiler_params=pltpu.CompilerParams(
            collective_id=0, has_side_effects=True, vmem_limit_bytes=40 * 1024 * 1024
        ),
    )(*operands)
    return state.reshape(species, levels, rows, cols), grad


def solution(mesh):
    in_specs = (
        P(None, None, ("gx", "gy")),
        P(None, ("gx", "gy"), None),
        P(None, ("gx", "gy")),
        P(None, ("gx", "gy")),
        P(None, "gx", "gy"),
        P(None, "gx", "gy"),
        P(None, "gx", "gy"),
        P(None, "gx", "gy"),
        P("gx", "gy"),
    )
    out_specs = (P(None, None, "gx", "gy"), P(None, ("gx", "gy")))
    body = functools.partial(local, mesh.shape["gx"], mesh.shape["gy"])
    return jax.shard_map(body, mesh=mesh, in_specs=in_specs, out_specs=out_specs, check_vma=False)
```

```python
import functools

import jax
import jax.numpy as jnp
from jax import lax
from jax.experimental import pallas as pl
from jax.experimental.pallas import tpu as pltpu
from jax.sharding import PartitionSpec as P

REG_DEV = 8
MESH = pl.DeviceIdType.MESH
F32 = jnp.float32
BF16 = jnp.bfloat16


def halves(value):
    high = value.astype(BF16)
    low = (value - high.astype(F32)).astype(BF16)
    return high, low


def dot_nt(a, b):
    return lax.dot_general(a, b, (((1,), (1,)), ((), ())), preferred_element_type=F32)


def kernel(
    dims,
    *refs,
):
    sources, refs = refs[:9], refs[9:]
    state, grad_ref = refs[:2]
    inside, refs = refs[2:11], refs[11:]
    adj_ref, owner_ref, column_ref, level_ref, wx_ref, wy_ref, diff_ref, prior_ref, region_ref = inside
    moves = list(zip(sources, inside))
    (
    table,
    send,
    recv,
    inv_ref,
    coup_ref,
    ratio_ref,
    forcing,
    forced,
    moved,
    row_out,
    row_in,
    col_out,
    col_in,
    surf,
    gsend,
    grecv,
    pix_send,
    pix_recv,
    halo_send,
    halo_recv,
    g_send,
    g_recv,
    in_sem,
    ) = refs
    nx, ny, species, levels, akl, steps, rows, cols, pixels, slots = dims
    n = nx * ny
    planes = species * levels
    width = species * akl + 8
    gx, gy = lax.axis_index("gx"), lax.axis_index("gy")
    me = gx * ny + gy

    def partner(dx, dy):
        px, py = gx + dx, gy + dy
        px = jnp.where(px >= nx, px - nx, px)
        py = jnp.where(py >= ny, py - ny, py)
        return px * ny + py, (px, py)

    turns = [(dx, dy) for dx in range(nx) for dy in range(ny)][1:]

    row_in[...] = jnp.zeros(row_in.shape, F32)
    col_in[...] = jnp.zeros(col_in.shape, F32)
    loads = [pltpu.make_async_copy(a, b, in_sem.at[i]) for i, (a, b) in enumerate(moves)]
    for load in loads:
        load.start()
    table[...] = jnp.zeros(table.shape, F32)
    barrier = pltpu.get_barrier_semaphore()

    for turn in turns:
        pl.semaphore_signal(barrier, inc=1, device_id=partner(*turn)[1], device_id_type=MESH)

    for i in range(4):
        loads[i].wait()

    def hits_of(k):
        owner = owner_ref[k : k + 1, :].astype(F32)
        along = jnp.broadcast_to(owner, (pixels, pixels))
        down = along.T
        first = lax.broadcasted_iota(jnp.int32, (pixels, pixels), 0)
        second = lax.broadcasted_iota(jnp.int32, (pixels, pixels), 1)
        earlier = jnp.where((along == down) & (first < second), 1.0, 0.0)
        slot = jnp.sum(earlier, axis=0, keepdims=True)
        position = (owner * slots + slot).astype(jnp.int32)
        place = lax.broadcasted_iota(jnp.int32, (n * slots, pixels), 0)
        return jnp.where(place == position, 1.0, 0.0).astype(BF16)

    def pack(t, group):
        for i, k in enumerate(group):
            at = width * i
            table[t, at : at + species * akl, i * pixels : (i + 1) * pixels] = adj_ref[k]
            at = at + species * akl
            codes = jnp.concatenate([column_ref[k : k + 1, :], level_ref[k : k + 1, :]], axis=0)
            table[t, at : at + 2, i * pixels : (i + 1) * pixels] = codes.astype(F32)
        hits = jnp.concatenate([hits_of(k) for k in group], axis=1)
        high, low = halves(table[t, :, : len(group) * pixels])
        send[t] = dot_nt(hits, high) + dot_nt(hits, low)

    def pixel_copy(t, turn):
        other, place = partner(*turn)
        return pltpu.make_async_remote_copy(
            src_ref=send.at[t, pl.ds(pl.multiple_of(other * slots, slots), slots)],
            dst_ref=recv.at[t, pl.ds(pl.multiple_of(me * slots, slots), slots)],
            send_sem=pix_send.at[t],
            recv_sem=pix_recv.at[t],
            device_id=place,
            device_id_type=MESH,
        )

    def pixel_all(t):
        part = pl.ds(0, (n - 1) * slots)
        return pltpu.make_async_remote_copy(
            src_ref=send.at[t, part],
            dst_ref=recv.at[t, part],
            send_sem=pix_send.at[t],
            recv_sem=pix_recv.at[t],
            device_id=partner(*turns[0])[1],
            device_id_type=MESH,
        )

    def send_pixels(t):
        for turn in turns:
            pixel_copy(t, turn).start()
        mine = pl.ds(pl.multiple_of(me * slots, slots), slots)
        recv[t, mine, :] = send[t, mine, :]

    pack(0, (steps - 1,))
    pl.semaphore_wait(barrier, n - 1)
    send_pixels(0)
    pack(1, tuple(range(steps - 1)))
    send_pixels(1)
    for load in loads[4:]:
        load.wait()

    ratio = jnp.zeros((rows, cols), F32)
    for level in range(levels):
        below = diff_ref[level - 1] if level else jnp.zeros((rows, cols), F32)
        above = diff_ref[level] if level < levels - 1 else jnp.zeros((rows, cols), F32)
        inverse = 1.0 / (1.0 + below + above + below * ratio)
        ratio = -above * inverse
        here = slice(level * rows, (level + 1) * rows)
        inv_ref[here, :] = inverse
        coup_ref[here, :] = below * inverse
        ratio_ref[here, :] = ratio
    surf[...] = jnp.zeros(surf.shape, F32)
    state[...] = jnp.zeros(state.shape, F32)

    lane = lax.broadcasted_iota(jnp.int32, (rows, cols), 1)
    sub = lax.broadcasted_iota(jnp.int32, (rows, cols), 0)

    def spread(t, k):
        if t == 0:
            pixel_all(0).wait_recv()
        total = [None] * rows
        chunk = min(256, n * slots)
        for first in range(0, n * slots, chunk):
            got = recv[t, first : first + chunk, :]
            if t:
                got = pltpu.roll(got, lax.rem(128 - width * k, 128), 1)
            spot = lax.broadcasted_iota(jnp.int32, got.shape, 1)
            column = jnp.broadcast_to(got[:, width - 8 : width - 7], got.shape).astype(jnp.int32)
            level = jnp.broadcast_to(got[:, width - 7 : width - 6], got.shape).astype(jnp.int32)
            profile = jnp.where(spot < akl, got, 0.0)
            for s in range(1, species):
                place = s * levels
                there = (spot >= place) & (spot < place + akl)
                profile = jnp.where(there, pltpu.roll(got, place - s * akl, 1), profile)
            bit = 1
            while bit <= levels - akl:
                profile = jnp.where((level & bit) != 0, pltpu.roll(profile, bit, 1), profile)
                bit *= 2
            high, low = halves(profile.T[:planes])
            both = jnp.concatenate([high, low], axis=0)
            for x in range(0, rows, 2):
                hits = jnp.concatenate(
                    [
                        jnp.where(column == spot + (x + d) * cols, 1.0, 0.0).astype(BF16)
                        for d in range(2)
                    ],
                    axis=1,
                )
                out = jnp.dot(both, hits, preferred_element_type=F32)
                out = out[:planes] + out[planes:]
                for d in range(2):
                    piece = out[:, d * cols : (d + 1) * cols]
                    total[x + d] = piece if total[x + d] is None else total[x + d] + piece
        for x in range(rows):
            forcing[pl.ds(x, planes, stride=rows), :] = total[x]

    has = (gx < nx - 1, gx > 0, gy < ny - 1, gy > 0)
    comes = (gx > 0, gx < nx - 1, gy > 0, gy < ny - 1)
    goes = (
        (jnp.minimum(gx + 1, nx - 1), gy),
        (jnp.maximum(gx - 1, 0), gy),
        (gx, jnp.minimum(gy + 1, ny - 1)),
        (gx, jnp.maximum(gy - 1, 0)),
    )

    def halo(k, side):
        source, target = (row_out, row_in) if side < 2 else (col_out, col_in)
        return pltpu.make_async_remote_copy(
            src_ref=source.at[k, side % 2],
            dst_ref=target.at[k, side % 2],
            send_sem=halo_send.at[k, side],
            recv_sem=halo_recv.at[k, side],
            device_id=goes[side],
            device_id_type=MESH,
        )

    spread(0, 0)

    def step(turn, carry):
        k = steps - 1 - turn
        wx, wy = wx_ref[k], wy_ref[k]
        ahead_x, back_x = jnp.maximum(-wx, 0.0), jnp.maximum(wx, 0.0)
        ahead_y, back_y = jnp.maximum(-wy, 0.0), jnp.maximum(wy, 0.0)
        forced[...] = state[...] + forcing[...]
        row_out[k, 0] = forced[pl.ds(rows - 1, planes, stride=rows), :] * ahead_x[rows - 1 : rows]
        row_out[k, 1] = forced[pl.ds(0, planes, stride=rows), :] * back_x[0:1]
        for side in (0, 1):
            pl.when(has[side])(lambda side=side: halo(k, side).start())
        up = jnp.zeros((rows, cols), F32)
        down = jnp.zeros((rows, cols), F32)
        for j in range(planes):
            cell = forced[j * rows : (j + 1) * rows, :]
            up = jnp.where(lane == j, pltpu.roll(ahead_y * cell, (j + 1) % cols, 1), up)
            down = jnp.where(lane == j, pltpu.roll(back_y * cell, j, 1) if j else back_y * cell, down)
        col_out[k, 0] = up
        col_out[k, 1] = down
        for side in (2, 3):
            pl.when(has[side])(lambda side=side: halo(k, side).start())
        remain = 1.0 - (ahead_x + back_x + ahead_y + back_y)
        ahead_x_in = jnp.where(sub > 0, pltpu.roll(ahead_x, 1, 0), 0.0)
        back_x_in = jnp.where(sub < rows - 1, pltpu.roll(back_x, rows - 1, 0), 0.0)
        ahead_y_in = jnp.where(lane > 0, pltpu.roll(ahead_y, 1, 1), 0.0)
        back_y_in = jnp.where(lane < cols - 1, pltpu.roll(back_y, cols - 1, 1), 0.0)
        for j in range(planes):
            cell = forced[j * rows : (j + 1) * rows, :]
            moved[j * rows : (j + 1) * rows, :] = (
                cell * remain
                + ahead_x_in * pltpu.roll(cell, 1, 0)
                + back_x_in * pltpu.roll(cell, rows - 1, 0)
                + ahead_y_in * pltpu.roll(cell, 1, 1)
                + back_y_in * pltpu.roll(cell, cols - 1, 1)
            )

        @pl.when(k > 0)
        def _():
            pl.when(k == steps - 1)(lambda: pixel_all(1).wait_recv())
            spread(1, jnp.maximum(k - 1, 0))

        for side in range(4):
            pl.when(comes[side])(lambda side=side: halo(k, side).wait_recv())
        moved[pl.ds(0, planes, stride=rows), :] += row_in[k, 0]
        moved[pl.ds(rows - 1, planes, stride=rows), :] += row_in[k, 1]
        up = col_in[k, 0]
        down = col_in[k, 1]
        for s in range(species):
            value = jnp.zeros((rows, cols), F32)
            for level in range(levels):
                j = s * levels + level
                here = slice(j * rows, (j + 1) * rows)
                flat = slice(level * rows, (level + 1) * rows)
                edge = jnp.where(lane == 0, pltpu.roll(up, (cols - j) % cols, 1) if j else up, 0.0)
                edge = jnp.where(lane == cols - 1, pltpu.roll(down, cols - 1 - j, 1), edge)
                value = (moved[here, :] + edge) * inv_ref[flat, :] + coup_ref[flat, :] * value
                moved[here, :] = value
            value = jnp.zeros((rows, cols), F32)
            for level in reversed(range(levels)):
                j = s * levels + level
                here = slice(j * rows, (j + 1) * rows)
                flat = slice(level * rows, (level + 1) * rows)
                value = moved[here, :] - ratio_ref[flat, :] * value
                state[here, :] = value
            surf[s] += prior_ref[s] * value
        return carry

    lax.fori_loop(0, steps, step, 0)

    region = region_ref[...]
    hits, parts = [], []
    sums = [surf[s] + pltpu.roll(surf[s], rows - 1, 0) for s in range(species)]
    for x in range(0, rows, 2):
        reg = region[x : x + 1]
        owner = lax.broadcasted_iota(jnp.int32, (n, cols), 0)
        hits.append(jnp.where(owner == lax.shift_right_logical(reg, 3), 1.0, 0.0).astype(BF16))
        place = lax.broadcasted_iota(jnp.int32, (REG_DEV, cols), 0)
        same = place == (reg & (REG_DEV - 1))
        blocks = [jnp.where(same, sums[s][x : x + 1], 0.0) for s in range(species)]
        blocks.append(jnp.zeros((128 - species * REG_DEV, cols), F32))
        parts.append(jnp.concatenate(blocks, axis=0))
    hits = jnp.concatenate(hits, axis=1)
    high, low = halves(jnp.concatenate(parts, axis=1))
    gsend[...] = (dot_nt(hits, high) + dot_nt(hits, low)).reshape(n, 1, 128)

    for turn in turns:
        other, place = partner(*turn)
        pltpu.make_async_remote_copy(
            src_ref=gsend.at[other],
            dst_ref=grecv.at[me],
            send_sem=g_send,
            recv_sem=g_recv,
            device_id=place,
            device_id_type=MESH,
        ).start()
    grecv[me] = gsend[me]
    for t in range(2):
        pixel_all(t).wait_send()
    for k in range(steps):
        for side in range(4):
            pl.when(has[side])(lambda side=side, k=k: halo(k, side).wait_send())
    everything = pltpu.make_async_remote_copy(
        src_ref=gsend.at[pl.ds(0, n - 1)],
        dst_ref=grecv.at[pl.ds(0, n - 1)],
        send_sem=g_send,
        recv_sem=g_recv,
        device_id=partner(*turns[0])[1],
        device_id_type=MESH,
    )
    everything.wait_send()
    everything.wait_recv()
    total = jnp.sum(grecv[...], axis=0)
    for s in range(species):
        grad_ref[s : s + 1, :] = total[:, s * REG_DEV : (s + 1) * REG_DEV]


def local(nx, ny, *args):
    adj, owner, column, level, wx, wy, diff, prior, region = args
    steps, rows, cols = wx.shape
    levels, species = diff.shape[0] + 1, prior.shape[0]
    pixels, akl = adj.shape[2], adj.shape[1] // species
    n = nx * ny
    slots = -(-(2 * pixels // n) // 8) * 8
    planes = species * levels
    dims = (nx, ny, species, levels, akl, steps, rows, cols, pixels, slots)
    vmem = pl.BlockSpec(memory_space=pltpu.VMEM)
    tile = (planes * rows, cols)
    operands = (adj, owner.reshape(steps, pixels), column, level, wx, wy, diff, prior, region)
    state, grad = pl.pallas_call(
        functools.partial(kernel, dims),
        out_shape=(
            jax.ShapeDtypeStruct(tile, F32),
            jax.ShapeDtypeStruct((species, REG_DEV), F32),
        ),
        in_specs=[pl.BlockSpec(memory_space=pltpu.HBM)] * 9,
        out_specs=(vmem, vmem),
        scratch_shapes=[
            *[pltpu.VMEM(a.shape, a.dtype) for a in operands],
            pltpu.VMEM((2, 128, (steps - 1) * pixels), F32),
            pltpu.VMEM((2, n * slots, 128), F32),
            pltpu.VMEM((2, n * slots, 128), F32),
            pltpu.VMEM((levels * rows, cols), F32),
            pltpu.VMEM((levels * rows, cols), F32),
            pltpu.VMEM((levels * rows, cols), F32),
            pltpu.VMEM(tile, F32),
            pltpu.VMEM(tile, F32),
            pltpu.VMEM(tile, F32),
            pltpu.VMEM((steps, 2, planes, cols), F32),
            pltpu.VMEM((steps, 2, planes, cols), F32),
            pltpu.VMEM((steps, 2, rows, cols), F32),
            pltpu.VMEM((steps, 2, rows, cols), F32),
            pltpu.VMEM((species, rows, cols), F32),
            pltpu.VMEM((n, 1, 128), F32),
            pltpu.VMEM((n, 1, 128), F32),
            pltpu.SemaphoreType.DMA((2,)),
            pltpu.SemaphoreType.DMA((2,)),
            pltpu.SemaphoreType.DMA((steps, 4)),
            pltpu.SemaphoreType.DMA((steps, 4)),
            pltpu.SemaphoreType.DMA,
            pltpu.SemaphoreType.DMA,
            pltpu.SemaphoreType.DMA((9,)),
        ],
        compiler_params=pltpu.CompilerParams(
            collective_id=0, has_side_effects=True, vmem_limit_bytes=56 * 1024 * 1024
        ),
    )(*operands)
    return state.reshape(species, levels, rows, cols), grad


def solution(mesh):
    in_specs = (
        P(None, None, ("gx", "gy")),
        P(None, ("gx", "gy"), None),
        P(None, ("gx", "gy")),
        P(None, ("gx", "gy")),
        P(None, "gx", "gy"),
        P(None, "gx", "gy"),
        P(None, "gx", "gy"),
        P(None, "gx", "gy"),
        P("gx", "gy"),
    )
    out_specs = (P(None, None, "gx", "gy"), P(None, ("gx", "gy")))
    body = functools.partial(local, mesh.shape["gx"], mesh.shape["gy"])
    return jax.shard_map(body, mesh=mesh, in_specs=in_specs, out_specs=out_specs, check_vma=False)
```

```python
import functools

import jax
import jax.numpy as jnp
from jax import lax
from jax.experimental import pallas as pl
from jax.experimental.pallas import tpu as pltpu
from jax.sharding import PartitionSpec as P

REG_DEV = 8
MESH = pl.DeviceIdType.MESH
F32 = jnp.float32
BF16 = jnp.bfloat16


def halves(value):
    high = value.astype(BF16)
    low = (value - high.astype(F32)).astype(BF16)
    return high, low


def dot_nt(a, b):
    return lax.dot_general(a, b, (((1,), (1,)), ((), ())), preferred_element_type=F32)


def kernel(
    dims,
    *refs,
):
    sources, refs = refs[:9], refs[9:]
    state, grad_ref = refs[:2]
    inside, refs = refs[2:11], refs[11:]
    adj_ref, owner_ref, column_ref, level_ref, wx_ref, wy_ref, diff_ref, prior_ref, region_ref = inside
    moves = list(zip(sources, inside))
    (
    table,
    send,
    recv,
    inv_ref,
    coup_ref,
    ratio_ref,
    forcing,
    forced,
    moved,
    row_out,
    row_in,
    col_out,
    col_in,
    surf,
    gsend,
    grecv,
    pix_send,
    pix_recv,
    halo_send,
    halo_recv,
    g_send,
    g_recv,
    in_sem,
    owners,
    ) = refs
    nx, ny, species, levels, akl, steps, rows, cols, pixels, slots = dims
    n = nx * ny
    planes = species * levels
    width = species * akl + 8
    gx, gy = lax.axis_index("gx"), lax.axis_index("gy")
    me = gx * ny + gy

    def partner(dx, dy):
        px, py = gx + dx, gy + dy
        px = jnp.where(px >= nx, px - nx, px)
        py = jnp.where(py >= ny, py - ny, py)
        return px * ny + py, (px, py)

    turns = [(dx, dy) for dx in range(nx) for dy in range(ny)][1:]

    row_in[...] = jnp.zeros(row_in.shape, F32)
    col_in[...] = jnp.zeros(col_in.shape, F32)
    loads = [pltpu.make_async_copy(a, b, in_sem.at[i]) for i, (a, b) in enumerate(moves)]
    for load in loads:
        load.start()
    barrier = pltpu.get_barrier_semaphore()

    for turn in turns:
        pl.semaphore_signal(barrier, inc=1, device_id=partner(*turn)[1], device_id_type=MESH)

    table[...] = jnp.zeros(table.shape, F32)
    for i in range(4):
        loads[i].wait()

    def hits_of(k):
        owner = owner_ref[k : k + 1, :].astype(F32)
        along = jnp.broadcast_to(owner, (pixels, pixels))
        down = along.T
        first = lax.broadcasted_iota(jnp.int32, (pixels, pixels), 0)
        second = lax.broadcasted_iota(jnp.int32, (pixels, pixels), 1)
        earlier = jnp.where((along == down) & (first < second), 1.0, 0.0)
        slot = jnp.sum(earlier, axis=0, keepdims=True)
        position = (owner * slots + slot).astype(jnp.int32)
        place = lax.broadcasted_iota(jnp.int32, (n * slots, pixels), 0)
        return jnp.where(place == position, 1.0, 0.0).astype(BF16)

    def pack(t, group):
        for i, k in enumerate(group):
            at = width * i
            table[t, at : at + species * akl, i * pixels : (i + 1) * pixels] = adj_ref[k]
            at = at + species * akl
            codes = jnp.concatenate([column_ref[k : k + 1, :], level_ref[k : k + 1, :]], axis=0)
            table[t, at : at + 2, i * pixels : (i + 1) * pixels] = codes.astype(F32)
        hits = jnp.concatenate([hits_of(k) for k in group], axis=1)
        high, low = halves(table[t, :, : len(group) * pixels])
        send[t] = dot_nt(hits, high) + dot_nt(hits, low)

    def pixel_copy(t, turn):
        other, place = partner(*turn)
        return pltpu.make_async_remote_copy(
            src_ref=send.at[t, pl.ds(pl.multiple_of(other * slots, slots), slots)],
            dst_ref=recv.at[t, pl.ds(pl.multiple_of(me * slots, slots), slots)],
            send_sem=pix_send.at[t],
            recv_sem=pix_recv.at[t],
            device_id=place,
            device_id_type=MESH,
        )

    def pixel_all(t):
        part = pl.ds(0, (n - 1) * slots)
        return pltpu.make_async_remote_copy(
            src_ref=send.at[t, part],
            dst_ref=recv.at[t, part],
            send_sem=pix_send.at[t],
            recv_sem=pix_recv.at[t],
            device_id=partner(*turns[0])[1],
            device_id_type=MESH,
        )

    def send_pixels(t):
        for turn in turns:
            pixel_copy(t, turn).start()
        mine = pl.ds(pl.multiple_of(me * slots, slots), slots)
        recv[t, mine, :] = send[t, mine, :]

    pack(0, (steps - 1,))
    pl.semaphore_wait(barrier, n - 1)
    send_pixels(0)
    pack(1, tuple(range(steps - 1)))
    send_pixels(1)
    def factor():
        ratio = jnp.zeros((rows, cols), F32)
        for level in range(levels):
            below = diff_ref[level - 1] if level else jnp.zeros((rows, cols), F32)
            above = diff_ref[level] if level < levels - 1 else jnp.zeros((rows, cols), F32)
            inverse = 1.0 / (1.0 + below + above + below * ratio)
            ratio = -above * inverse
            here = slice(level * rows, (level + 1) * rows)
            inv_ref[here, :] = inverse
            coup_ref[here, :] = below * inverse
            ratio_ref[here, :] = ratio

    def region_owners():
        device = lax.broadcasted_iota(jnp.int32, (n, cols), 0)
        for x in range(0, rows, 2):
            owner = lax.shift_right_logical(region_ref[x : x + 1], 3)
            hits = jnp.where(device == owner, 1.0, 0.0).astype(BF16)
            owners[:, x // 2 * cols : (x // 2 + 1) * cols] = hits

    for load in loads[4:]:
        load.wait()

    surf[...] = jnp.zeros(surf.shape, F32)
    state[...] = jnp.zeros(state.shape, F32)

    lane = lax.broadcasted_iota(jnp.int32, (rows, cols), 1)
    sub = lax.broadcasted_iota(jnp.int32, (rows, cols), 0)

    def spread(t, k):
        if t == 0:
            pixel_all(0).wait_recv()
        total = [None] * rows
        chunk = min(256, n * slots)
        for first in range(0, n * slots, chunk):
            got = recv[t, first : first + chunk, :]
            if t:
                got = pltpu.roll(got, lax.rem(128 - width * k, 128), 1)
            spot = lax.broadcasted_iota(jnp.int32, got.shape, 1)
            column = jnp.broadcast_to(got[:, width - 8 : width - 7], got.shape).astype(jnp.int32)
            level = jnp.broadcast_to(got[:, width - 7 : width - 6], got.shape).astype(jnp.int32)
            profile = jnp.where(spot < akl, got, 0.0)
            for s in range(1, species):
                place = s * levels
                there = (spot >= place) & (spot < place + akl)
                profile = jnp.where(there, pltpu.roll(got, place - s * akl, 1), profile)
            bit = 1
            while bit <= levels - akl:
                profile = jnp.where((level & bit) != 0, pltpu.roll(profile, bit, 1), profile)
                bit *= 2
            high, low = halves(profile.T[:planes])
            both = jnp.concatenate([high, low], axis=0)
            for x in range(0, rows, 2):
                hits = jnp.concatenate(
                    [
                        jnp.where(column == spot + (x + d) * cols, 1.0, 0.0).astype(BF16)
                        for d in range(2)
                    ],
                    axis=1,
                )
                out = jnp.dot(both, hits, preferred_element_type=F32)
                out = out[:planes] + out[planes:]
                for d in range(2):
                    piece = out[:, d * cols : (d + 1) * cols]
                    total[x + d] = piece if total[x + d] is None else total[x + d] + piece
        for x in range(rows):
            forcing[pl.ds(x, planes, stride=rows), :] = total[x]

    has = (gx < nx - 1, gx > 0, gy < ny - 1, gy > 0)
    comes = (gx > 0, gx < nx - 1, gy > 0, gy < ny - 1)
    goes = (
        (jnp.minimum(gx + 1, nx - 1), gy),
        (jnp.maximum(gx - 1, 0), gy),
        (gx, jnp.minimum(gy + 1, ny - 1)),
        (gx, jnp.maximum(gy - 1, 0)),
    )

    def halo(k, side):
        source, target = (row_out, row_in) if side < 2 else (col_out, col_in)
        return pltpu.make_async_remote_copy(
            src_ref=source.at[k, side % 2],
            dst_ref=target.at[k, side % 2],
            send_sem=halo_send.at[k, side],
            recv_sem=halo_recv.at[k, side],
            device_id=goes[side],
            device_id_type=MESH,
        )

    spread(0, 0)

    def step(turn, carry):
        k = steps - 1 - turn
        wx, wy = wx_ref[k], wy_ref[k]
        ahead_x, back_x = jnp.maximum(-wx, 0.0), jnp.maximum(wx, 0.0)
        ahead_y, back_y = jnp.maximum(-wy, 0.0), jnp.maximum(wy, 0.0)
        forced[...] = state[...] + forcing[...]
        row_out[k, 0] = forced[pl.ds(rows - 1, planes, stride=rows), :] * ahead_x[rows - 1 : rows]
        row_out[k, 1] = forced[pl.ds(0, planes, stride=rows), :] * back_x[0:1]
        for side in (0, 1):
            pl.when(has[side])(lambda side=side: halo(k, side).start())
        up = jnp.zeros((rows, cols), F32)
        down = jnp.zeros((rows, cols), F32)
        for j in range(planes):
            cell = forced[j * rows : (j + 1) * rows, :]
            up = jnp.where(lane == j, pltpu.roll(ahead_y * cell, (j + 1) % cols, 1), up)
            down = jnp.where(lane == j, pltpu.roll(back_y * cell, j, 1) if j else back_y * cell, down)
        col_out[k, 0] = up
        col_out[k, 1] = down
        for side in (2, 3):
            pl.when(has[side])(lambda side=side: halo(k, side).start())
        remain = 1.0 - (ahead_x + back_x + ahead_y + back_y)
        ahead_x_in = jnp.where(sub > 0, pltpu.roll(ahead_x, 1, 0), 0.0)
        back_x_in = jnp.where(sub < rows - 1, pltpu.roll(back_x, rows - 1, 0), 0.0)
        ahead_y_in = jnp.where(lane > 0, pltpu.roll(ahead_y, 1, 1), 0.0)
        back_y_in = jnp.where(lane < cols - 1, pltpu.roll(back_y, cols - 1, 1), 0.0)
        for j in range(planes):
            cell = forced[j * rows : (j + 1) * rows, :]
            moved[j * rows : (j + 1) * rows, :] = (
                cell * remain
                + ahead_x_in * pltpu.roll(cell, 1, 0)
                + back_x_in * pltpu.roll(cell, rows - 1, 0)
                + ahead_y_in * pltpu.roll(cell, 1, 1)
                + back_y_in * pltpu.roll(cell, cols - 1, 1)
            )

        @pl.when(k > 0)
        def _():
            pl.when(k == steps - 1)(factor)
            pl.when(k == steps - 2)(region_owners)
            pl.when(k == steps - 1)(lambda: pixel_all(1).wait_recv())
            spread(1, jnp.maximum(k - 1, 0))

        for side in range(4):
            pl.when(comes[side])(lambda side=side: halo(k, side).wait_recv())
        moved[pl.ds(0, planes, stride=rows), :] += row_in[k, 0]
        moved[pl.ds(rows - 1, planes, stride=rows), :] += row_in[k, 1]
        up = col_in[k, 0]
        down = col_in[k, 1]
        for s in range(species):
            value = jnp.zeros((rows, cols), F32)
            for level in range(levels):
                j = s * levels + level
                here = slice(j * rows, (j + 1) * rows)
                flat = slice(level * rows, (level + 1) * rows)
                edge = jnp.where(lane == 0, pltpu.roll(up, (cols - j) % cols, 1) if j else up, 0.0)
                edge = jnp.where(lane == cols - 1, pltpu.roll(down, cols - 1 - j, 1), edge)
                value = (moved[here, :] + edge) * inv_ref[flat, :] + coup_ref[flat, :] * value
                moved[here, :] = value
            value = jnp.zeros((rows, cols), F32)
            for level in reversed(range(levels)):
                j = s * levels + level
                here = slice(j * rows, (j + 1) * rows)
                flat = slice(level * rows, (level + 1) * rows)
                value = moved[here, :] - ratio_ref[flat, :] * value
                state[here, :] = value
            surf[s] += prior_ref[s] * value
        return carry

    lax.fori_loop(0, steps, step, 0)

    region = region_ref[...]
    parts = []
    sums = [surf[s] + pltpu.roll(surf[s], rows - 1, 0) for s in range(species)]
    for x in range(0, rows, 2):
        reg = region[x : x + 1]
        place = lax.broadcasted_iota(jnp.int32, (REG_DEV, cols), 0)
        same = place == (reg & (REG_DEV - 1))
        blocks = [jnp.where(same, sums[s][x : x + 1], 0.0) for s in range(species)]
        blocks.append(jnp.zeros((128 - species * REG_DEV, cols), F32))
        parts.append(jnp.concatenate(blocks, axis=0))
    hits = owners[...]
    high, low = halves(jnp.concatenate(parts, axis=1))
    gsend[...] = (dot_nt(hits, high) + dot_nt(hits, low)).reshape(n, 1, 128)

    for turn in turns:
        other, place = partner(*turn)
        pltpu.make_async_remote_copy(
            src_ref=gsend.at[other],
            dst_ref=grecv.at[me],
            send_sem=g_send,
            recv_sem=g_recv,
            device_id=place,
            device_id_type=MESH,
        ).start()
    grecv[me] = gsend[me]
    for t in range(2):
        pixel_all(t).wait_send()
    for k in range(steps):
        for side in range(4):
            pl.when(has[side])(lambda side=side, k=k: halo(k, side).wait_send())
    everything = pltpu.make_async_remote_copy(
        src_ref=gsend.at[pl.ds(0, n - 1)],
        dst_ref=grecv.at[pl.ds(0, n - 1)],
        send_sem=g_send,
        recv_sem=g_recv,
        device_id=partner(*turns[0])[1],
        device_id_type=MESH,
    )
    everything.wait_send()
    everything.wait_recv()
    total = jnp.sum(grecv[...], axis=0)
    for s in range(species):
        grad_ref[s : s + 1, :] = total[:, s * REG_DEV : (s + 1) * REG_DEV]


def local(nx, ny, *args):
    adj, owner, column, level, wx, wy, diff, prior, region = args
    steps, rows, cols = wx.shape
    levels, species = diff.shape[0] + 1, prior.shape[0]
    pixels, akl = adj.shape[2], adj.shape[1] // species
    n = nx * ny
    slots = -(-(2 * pixels // n) // 8) * 8
    planes = species * levels
    dims = (nx, ny, species, levels, akl, steps, rows, cols, pixels, slots)
    vmem = pl.BlockSpec(memory_space=pltpu.VMEM)
    tile = (planes * rows, cols)
    operands = (adj, owner.reshape(steps, pixels), column, level, wx, wy, diff, prior, region)
    state, grad = pl.pallas_call(
        functools.partial(kernel, dims),
        out_shape=(
            jax.ShapeDtypeStruct(tile, F32),
            jax.ShapeDtypeStruct((species, REG_DEV), F32),
        ),
        in_specs=[pl.BlockSpec(memory_space=pltpu.HBM)] * 9,
        out_specs=(vmem, vmem),
        scratch_shapes=[
            *[pltpu.VMEM(a.shape, a.dtype) for a in operands],
            pltpu.VMEM((2, 128, (steps - 1) * pixels), F32),
            pltpu.VMEM((2, n * slots, 128), F32),
            pltpu.VMEM((2, n * slots, 128), F32),
            pltpu.VMEM((levels * rows, cols), F32),
            pltpu.VMEM((levels * rows, cols), F32),
            pltpu.VMEM((levels * rows, cols), F32),
            pltpu.VMEM(tile, F32),
            pltpu.VMEM(tile, F32),
            pltpu.VMEM(tile, F32),
            pltpu.VMEM((steps, 2, planes, cols), F32),
            pltpu.VMEM((steps, 2, planes, cols), F32),
            pltpu.VMEM((steps, 2, rows, cols), F32),
            pltpu.VMEM((steps, 2, rows, cols), F32),
            pltpu.VMEM((species, rows, cols), F32),
            pltpu.VMEM((n, 1, 128), F32),
            pltpu.VMEM((n, 1, 128), F32),
            pltpu.SemaphoreType.DMA((2,)),
            pltpu.SemaphoreType.DMA((2,)),
            pltpu.SemaphoreType.DMA((steps, 4)),
            pltpu.SemaphoreType.DMA((steps, 4)),
            pltpu.SemaphoreType.DMA,
            pltpu.SemaphoreType.DMA,
            pltpu.SemaphoreType.DMA((9,)),
            pltpu.VMEM((n, rows // 2 * cols), BF16),
        ],
        compiler_params=pltpu.CompilerParams(
            collective_id=0, has_side_effects=True, vmem_limit_bytes=56 * 1024 * 1024
        ),
    )(*operands)
    return state.reshape(species, levels, rows, cols), grad


def solution(mesh):
    in_specs = (
        P(None, None, ("gx", "gy")),
        P(None, ("gx", "gy"), None),
        P(None, ("gx", "gy")),
        P(None, ("gx", "gy")),
        P(None, "gx", "gy"),
        P(None, "gx", "gy"),
        P(None, "gx", "gy"),
        P(None, "gx", "gy"),
        P("gx", "gy"),
    )
    out_specs = (P(None, None, "gx", "gy"), P(None, ("gx", "gy")))
    body = functools.partial(local, mesh.shape["gx"], mesh.shape["gy"])
    return jax.shard_map(body, mesh=mesh, in_specs=in_specs, out_specs=out_specs, check_vma=False)
```

```python
import functools

import jax
import jax.numpy as jnp
from jax import lax
from jax.experimental import pallas as pl
from jax.experimental.pallas import tpu as pltpu
from jax.sharding import PartitionSpec as P

REG_DEV = 8
MESH = pl.DeviceIdType.MESH
F32 = jnp.float32
BF16 = jnp.bfloat16


def halves(value):
    high = value.astype(BF16)
    low = (value - high.astype(F32)).astype(BF16)
    return high, low


def dot_nt(a, b):
    return lax.dot_general(a, b, (((1,), (1,)), ((), ())), preferred_element_type=F32)


def kernel(
    dims,
    *refs,
):
    sources, refs = refs[:9], refs[9:]
    state, grad_ref = refs[:2]
    inside, refs = refs[2:11], refs[11:]
    adj_ref, owner_ref, column_ref, level_ref, wx_ref, wy_ref, diff_ref, prior_ref, region_ref = inside
    moves = list(zip(sources, inside))
    (
    table,
    send,
    recv,
    inv_ref,
    coup_ref,
    ratio_ref,
    forcing,
    forced,
    moved,
    row_out,
    row_in,
    col_out,
    col_in,
    surf,
    gsend,
    grecv,
    pix_send,
    pix_recv,
    halo_send,
    halo_recv,
    g_send,
    g_recv,
    in_sem,
    owners,
    ) = refs
    nx, ny, species, levels, akl, steps, rows, cols, pixels, slots = dims
    n = nx * ny
    planes = species * levels
    width = species * akl + 8
    gx, gy = lax.axis_index("gx"), lax.axis_index("gy")
    me = gx * ny + gy

    def partner(dx, dy):
        px, py = gx + dx, gy + dy
        px = jnp.where(px >= nx, px - nx, px)
        py = jnp.where(py >= ny, py - ny, py)
        return px * ny + py, (px, py)

    turns = [(dx, dy) for dx in range(nx) for dy in range(ny)][1:]

    row_in[...] = jnp.zeros(row_in.shape, F32)
    col_in[...] = jnp.zeros(col_in.shape, F32)
    loads = [pltpu.make_async_copy(a, b, in_sem.at[i]) for i, (a, b) in enumerate(moves)]
    for load in loads:
        load.start()
    barrier = pltpu.get_barrier_semaphore()

    for turn in turns:
        pl.semaphore_signal(barrier, inc=1, device_id=partner(*turn)[1], device_id_type=MESH)

    table[...] = jnp.zeros(table.shape, F32)
    for i in range(4):
        loads[i].wait()

    def hits_of(k):
        owner = owner_ref[k : k + 1, :].astype(F32)
        along = jnp.broadcast_to(owner, (pixels, pixels))
        down = along.T
        first = lax.broadcasted_iota(jnp.int32, (pixels, pixels), 0)
        second = lax.broadcasted_iota(jnp.int32, (pixels, pixels), 1)
        earlier = jnp.where((along == down) & (first < second), 1.0, 0.0)
        slot = jnp.sum(earlier, axis=0, keepdims=True)
        position = (owner * slots + slot).astype(jnp.int32)
        place = lax.broadcasted_iota(jnp.int32, (n * slots, pixels), 0)
        return jnp.where(place == position, 1.0, 0.0).astype(BF16)

    def pack(t, group):
        for i, k in enumerate(group):
            at = width * i
            table[t, at : at + species * akl, i * pixels : (i + 1) * pixels] = adj_ref[k]
            at = at + species * akl
            codes = jnp.concatenate([column_ref[k : k + 1, :], level_ref[k : k + 1, :]], axis=0)
            table[t, at : at + 2, i * pixels : (i + 1) * pixels] = codes.astype(F32)
        hits = jnp.concatenate([hits_of(k) for k in group], axis=1)
        high, low = halves(table[t, :, : len(group) * pixels])
        send[t] = dot_nt(hits, high) + dot_nt(hits, low)

    def pixel_copy(t, turn):
        other, place = partner(*turn)
        return pltpu.make_async_remote_copy(
            src_ref=send.at[t, pl.ds(pl.multiple_of(other * slots, slots), slots)],
            dst_ref=recv.at[t, pl.ds(pl.multiple_of(me * slots, slots), slots)],
            send_sem=pix_send.at[t],
            recv_sem=pix_recv.at[t],
            device_id=place,
            device_id_type=MESH,
        )

    def pixel_all(t):
        part = pl.ds(0, (n - 1) * slots)
        return pltpu.make_async_remote_copy(
            src_ref=send.at[t, part],
            dst_ref=recv.at[t, part],
            send_sem=pix_send.at[t],
            recv_sem=pix_recv.at[t],
            device_id=partner(*turns[0])[1],
            device_id_type=MESH,
        )

    def send_pixels(t):
        for turn in turns:
            pixel_copy(t, turn).start()
        mine = pl.ds(pl.multiple_of(me * slots, slots), slots)
        recv[t, mine, :] = send[t, mine, :]

    pack(0, (steps - 1,))
    pack(1, tuple(range(steps - 1)))
    pl.semaphore_wait(barrier, n - 1)
    send_pixels(0)
    send_pixels(1)
    def factor():
        ratio = jnp.zeros((rows, cols), F32)
        for level in range(levels):
            below = diff_ref[level - 1] if level else jnp.zeros((rows, cols), F32)
            above = diff_ref[level] if level < levels - 1 else jnp.zeros((rows, cols), F32)
            inverse = 1.0 / (1.0 + below + above + below * ratio)
            ratio = -above * inverse
            here = slice(level * rows, (level + 1) * rows)
            inv_ref[here, :] = inverse
            coup_ref[here, :] = below * inverse
            ratio_ref[here, :] = ratio

    def region_owners():
        device = lax.broadcasted_iota(jnp.int32, (n, cols), 0)
        for x in range(0, rows, 2):
            owner = lax.shift_right_logical(region_ref[x : x + 1], 3)
            hits = jnp.where(device == owner, 1.0, 0.0).astype(BF16)
            owners[:, x // 2 * cols : (x // 2 + 1) * cols] = hits

    for load in loads[4:]:
        load.wait()

    surf[...] = jnp.zeros(surf.shape, F32)
    state[...] = jnp.zeros(state.shape, F32)

    lane = lax.broadcasted_iota(jnp.int32, (rows, cols), 1)
    sub = lax.broadcasted_iota(jnp.int32, (rows, cols), 0)

    def spread(t, k):
        if t == 0:
            pixel_all(0).wait_recv()
        total = [None] * rows
        chunk = min(256, n * slots)
        for first in range(0, n * slots, chunk):
            got = recv[t, first : first + chunk, :]
            if t:
                got = pltpu.roll(got, lax.rem(128 - width * k, 128), 1)
            spot = lax.broadcasted_iota(jnp.int32, got.shape, 1)
            column = jnp.broadcast_to(got[:, width - 8 : width - 7], got.shape).astype(jnp.int32)
            level = jnp.broadcast_to(got[:, width - 7 : width - 6], got.shape).astype(jnp.int32)
            profile = jnp.where(spot < akl, got, 0.0)
            for s in range(1, species):
                place = s * levels
                there = (spot >= place) & (spot < place + akl)
                profile = jnp.where(there, pltpu.roll(got, place - s * akl, 1), profile)
            bit = 1
            while bit <= levels - akl:
                profile = jnp.where((level & bit) != 0, pltpu.roll(profile, bit, 1), profile)
                bit *= 2
            high, low = halves(profile.T[:planes])
            both = jnp.concatenate([high, low], axis=0)
            for x in range(0, rows, 2):
                hits = jnp.concatenate(
                    [
                        jnp.where(column == spot + (x + d) * cols, 1.0, 0.0).astype(BF16)
                        for d in range(2)
                    ],
                    axis=1,
                )
                out = jnp.dot(both, hits, preferred_element_type=F32)
                out = out[:planes] + out[planes:]
                for d in range(2):
                    piece = out[:, d * cols : (d + 1) * cols]
                    total[x + d] = piece if total[x + d] is None else total[x + d] + piece
        for x in range(rows):
            forcing[pl.ds(x, planes, stride=rows), :] = total[x]

    has = (gx < nx - 1, gx > 0, gy < ny - 1, gy > 0)
    comes = (gx > 0, gx < nx - 1, gy > 0, gy < ny - 1)
    goes = (
        (jnp.minimum(gx + 1, nx - 1), gy),
        (jnp.maximum(gx - 1, 0), gy),
        (gx, jnp.minimum(gy + 1, ny - 1)),
        (gx, jnp.maximum(gy - 1, 0)),
    )

    def halo(k, side):
        source, target = (row_out, row_in) if side < 2 else (col_out, col_in)
        return pltpu.make_async_remote_copy(
            src_ref=source.at[k, side % 2],
            dst_ref=target.at[k, side % 2],
            send_sem=halo_send.at[k, side],
            recv_sem=halo_recv.at[k, side],
            device_id=goes[side],
            device_id_type=MESH,
        )

    spread(0, 0)

    def step(turn, carry):
        k = steps - 1 - turn
        wx, wy = wx_ref[k], wy_ref[k]
        ahead_x, back_x = jnp.maximum(-wx, 0.0), jnp.maximum(wx, 0.0)
        ahead_y, back_y = jnp.maximum(-wy, 0.0), jnp.maximum(wy, 0.0)
        forced[...] = state[...] + forcing[...]
        row_out[k, 0] = forced[pl.ds(rows - 1, planes, stride=rows), :] * ahead_x[rows - 1 : rows]
        row_out[k, 1] = forced[pl.ds(0, planes, stride=rows), :] * back_x[0:1]
        for side in (0, 1):
            pl.when(has[side])(lambda side=side: halo(k, side).start())
        up = jnp.zeros((rows, cols), F32)
        down = jnp.zeros((rows, cols), F32)
        for j in range(planes):
            cell = forced[j * rows : (j + 1) * rows, :]
            up = jnp.where(lane == j, pltpu.roll(ahead_y * cell, (j + 1) % cols, 1), up)
            down = jnp.where(lane == j, pltpu.roll(back_y * cell, j, 1) if j else back_y * cell, down)
        col_out[k, 0] = up
        col_out[k, 1] = down
        for side in (2, 3):
            pl.when(has[side])(lambda side=side: halo(k, side).start())
        remain = 1.0 - (ahead_x + back_x + ahead_y + back_y)
        ahead_x_in = jnp.where(sub > 0, pltpu.roll(ahead_x, 1, 0), 0.0)
        back_x_in = jnp.where(sub < rows - 1, pltpu.roll(back_x, rows - 1, 0), 0.0)
        ahead_y_in = jnp.where(lane > 0, pltpu.roll(ahead_y, 1, 1), 0.0)
        back_y_in = jnp.where(lane < cols - 1, pltpu.roll(back_y, cols - 1, 1), 0.0)
        for j in range(planes):
            cell = forced[j * rows : (j + 1) * rows, :]
            moved[j * rows : (j + 1) * rows, :] = (
                cell * remain
                + ahead_x_in * pltpu.roll(cell, 1, 0)
                + back_x_in * pltpu.roll(cell, rows - 1, 0)
                + ahead_y_in * pltpu.roll(cell, 1, 1)
                + back_y_in * pltpu.roll(cell, cols - 1, 1)
            )

        @pl.when(k > 0)
        def _():
            pl.when(k == steps - 1)(factor)
            pl.when(k == steps - 2)(region_owners)
            pl.when(k == steps - 1)(lambda: pixel_all(1).wait_recv())
            spread(1, jnp.maximum(k - 1, 0))

        for side in range(4):
            pl.when(comes[side])(lambda side=side: halo(k, side).wait_recv())
        moved[pl.ds(0, planes, stride=rows), :] += row_in[k, 0]
        moved[pl.ds(rows - 1, planes, stride=rows), :] += row_in[k, 1]
        up = col_in[k, 0]
        down = col_in[k, 1]
        for s in range(species):
            value = jnp.zeros((rows, cols), F32)
            for level in range(levels):
                j = s * levels + level
                here = slice(j * rows, (j + 1) * rows)
                flat = slice(level * rows, (level + 1) * rows)
                edge = jnp.where(lane == 0, pltpu.roll(up, (cols - j) % cols, 1) if j else up, 0.0)
                edge = jnp.where(lane == cols - 1, pltpu.roll(down, cols - 1 - j, 1), edge)
                value = (moved[here, :] + edge) * inv_ref[flat, :] + coup_ref[flat, :] * value
                moved[here, :] = value
            value = jnp.zeros((rows, cols), F32)
            for level in reversed(range(levels)):
                j = s * levels + level
                here = slice(j * rows, (j + 1) * rows)
                flat = slice(level * rows, (level + 1) * rows)
                value = moved[here, :] - ratio_ref[flat, :] * value
                state[here, :] = value
            surf[s] += prior_ref[s] * value
        return carry

    lax.fori_loop(0, steps, step, 0)

    region = region_ref[...]
    parts = []
    sums = [surf[s] + pltpu.roll(surf[s], rows - 1, 0) for s in range(species)]
    for x in range(0, rows, 2):
        reg = region[x : x + 1]
        place = lax.broadcasted_iota(jnp.int32, (REG_DEV, cols), 0)
        same = place == (reg & (REG_DEV - 1))
        blocks = [jnp.where(same, sums[s][x : x + 1], 0.0) for s in range(species)]
        blocks.append(jnp.zeros((128 - species * REG_DEV, cols), F32))
        parts.append(jnp.concatenate(blocks, axis=0))
    hits = owners[...]
    high, low = halves(jnp.concatenate(parts, axis=1))
    gsend[...] = (dot_nt(hits, high) + dot_nt(hits, low)).reshape(n, 1, 128)

    for turn in turns:
        other, place = partner(*turn)
        pltpu.make_async_remote_copy(
            src_ref=gsend.at[other],
            dst_ref=grecv.at[me],
            send_sem=g_send,
            recv_sem=g_recv,
            device_id=place,
            device_id_type=MESH,
        ).start()
    grecv[me] = gsend[me]
    for t in range(2):
        pixel_all(t).wait_send()
    for k in range(steps):
        for side in range(4):
            pl.when(has[side])(lambda side=side, k=k: halo(k, side).wait_send())
    everything = pltpu.make_async_remote_copy(
        src_ref=gsend.at[pl.ds(0, n - 1)],
        dst_ref=grecv.at[pl.ds(0, n - 1)],
        send_sem=g_send,
        recv_sem=g_recv,
        device_id=partner(*turns[0])[1],
        device_id_type=MESH,
    )
    everything.wait_send()
    everything.wait_recv()
    total = jnp.sum(grecv[...], axis=0)
    for s in range(species):
        grad_ref[s : s + 1, :] = total[:, s * REG_DEV : (s + 1) * REG_DEV]


def local(nx, ny, *args):
    adj, owner, column, level, wx, wy, diff, prior, region = args
    steps, rows, cols = wx.shape
    levels, species = diff.shape[0] + 1, prior.shape[0]
    pixels, akl = adj.shape[2], adj.shape[1] // species
    n = nx * ny
    slots = -(-(2 * pixels // n) // 8) * 8
    planes = species * levels
    dims = (nx, ny, species, levels, akl, steps, rows, cols, pixels, slots)
    vmem = pl.BlockSpec(memory_space=pltpu.VMEM)
    tile = (planes * rows, cols)
    operands = (adj, owner.reshape(steps, pixels), column, level, wx, wy, diff, prior, region)
    state, grad = pl.pallas_call(
        functools.partial(kernel, dims),
        out_shape=(
            jax.ShapeDtypeStruct(tile, F32),
            jax.ShapeDtypeStruct((species, REG_DEV), F32),
        ),
        in_specs=[pl.BlockSpec(memory_space=pltpu.HBM)] * 9,
        out_specs=(vmem, vmem),
        scratch_shapes=[
            *[pltpu.VMEM(a.shape, a.dtype) for a in operands],
            pltpu.VMEM((2, 128, (steps - 1) * pixels), F32),
            pltpu.VMEM((2, n * slots, 128), F32),
            pltpu.VMEM((2, n * slots, 128), F32),
            pltpu.VMEM((levels * rows, cols), F32),
            pltpu.VMEM((levels * rows, cols), F32),
            pltpu.VMEM((levels * rows, cols), F32),
            pltpu.VMEM(tile, F32),
            pltpu.VMEM(tile, F32),
            pltpu.VMEM(tile, F32),
            pltpu.VMEM((steps, 2, planes, cols), F32),
            pltpu.VMEM((steps, 2, planes, cols), F32),
            pltpu.VMEM((steps, 2, rows, cols), F32),
            pltpu.VMEM((steps, 2, rows, cols), F32),
            pltpu.VMEM((species, rows, cols), F32),
            pltpu.VMEM((n, 1, 128), F32),
            pltpu.VMEM((n, 1, 128), F32),
            pltpu.SemaphoreType.DMA((2,)),
            pltpu.SemaphoreType.DMA((2,)),
            pltpu.SemaphoreType.DMA((steps, 4)),
            pltpu.SemaphoreType.DMA((steps, 4)),
            pltpu.SemaphoreType.DMA,
            pltpu.SemaphoreType.DMA,
            pltpu.SemaphoreType.DMA((9,)),
            pltpu.VMEM((n, rows // 2 * cols), BF16),
        ],
        compiler_params=pltpu.CompilerParams(
            collective_id=0, has_side_effects=True, vmem_limit_bytes=56 * 1024 * 1024
        ),
    )(*operands)
    return state.reshape(species, levels, rows, cols), grad


def solution(mesh):
    in_specs = (
        P(None, None, ("gx", "gy")),
        P(None, ("gx", "gy"), None),
        P(None, ("gx", "gy")),
        P(None, ("gx", "gy")),
        P(None, "gx", "gy"),
        P(None, "gx", "gy"),
        P(None, "gx", "gy"),
        P(None, "gx", "gy"),
        P("gx", "gy"),
    )
    out_specs = (P(None, None, "gx", "gy"), P(None, ("gx", "gy")))
    body = functools.partial(local, mesh.shape["gx"], mesh.shape["gy"])
    return jax.shard_map(body, mesh=mesh, in_specs=in_specs, out_specs=out_specs, check_vma=False)
```
